256 devices in a mesh: cuts: 32 (over z, y_hi, core), col: 8 (over y_lo, x).
Axes of the slice: x: 4, y: 4 (y_hi: 2, y_lo: 2; y = y_hi * 2 + y_lo), z: 8, core: 2. Of those that a mesh axis runs over, the one named last changes fastest.
Arguments:
- lower: bfloat16 [16, 32, 512, 512], P('col', 'cuts'), may hold values from -0.109375 to 0.109375
- upper: bfloat16 [16, 32, 512, 512], P('col', 'cuts'), may hold values from -0.109375 to 0.109375
- rhs: bfloat16 [16, 32, 512, 512], P('col', 'cuts'), may hold values from -6 to 6
Outputs:
- reduced: float32 [16, 32, 512, 512], P('col', 'cuts')
The draws below stay inside these ranges and needn't reach their ends.
All inputs are finite; a program needn't handle non-finite values.
Results may differ from the reference program's by a relative error of at most 0.0051.
Values may be sent and summed in bfloat16 or wider, within the bound.
A program may use at most 128 MiB of HBM per device.

```python
import jax
import jax.numpy as jnp

W = 512
K = 512
ROWS = 16
LANES = 32


def shard_levels(key, extent, shards, low, high):
    level = 1.0
    for position, blocks in shards:
        draws = jax.random.uniform(jax.random.fold_in(jax.random.fold_in(key, 6), position), (blocks,), jnp.float32, low / len(shards), high / len(shards))
        level = level * jnp.repeat(jnp.exp(draws), extent[position] // blocks).reshape((-1,) + (1,) * (len(extent) - 1 - position))
    return level


def centred(key, extent, width, bound, pieces=(), kind=jnp.bfloat16):
    gain = shard_levels(key, extent, pieces, -0.22, 0.18) if pieces else 1.0
    drawn = jax.random.normal(key, extent, jnp.float32) * width * gain
    return jnp.minimum(jnp.maximum(drawn, -bound), bound).astype(kind)


def setup_inputs(seed: int = 0) -> dict:
    splits = jax.random.split(jax.random.key(seed), 4)
    return {
        "lower": centred(splits[0], (ROWS, LANES, W, W), (6 * W) ** -0.5, 0.109375, ((0, 8), (1, 32))),
        "upper": centred(splits[1], (ROWS, LANES, W, W), (6 * W) ** -0.5, 0.109375, ((0, 8), (1, 32))),
        "rhs": centred(splits[2], (ROWS, LANES, W, K), 1.0, 6.0, ((0, 8), (1, 32))),
    }


def batch_product(left, right):
    return jnp.einsum("sij,sjk->sik", left.astype(jnp.float32), right.astype(jnp.float32))


def from_below(values, shift_by):
    zeros = jnp.zeros((shift_by,) + values.shape[1:], values.dtype)
    return jnp.concatenate([zeros, values[:-shift_by]], axis=0)


def from_above(values, shift_by):
    zeros = jnp.zeros((shift_by,) + values.shape[1:], values.dtype)
    return jnp.concatenate([values[shift_by:], zeros], axis=0)


def horner(correction, values):
    first = (values + batch_product(correction, values)).astype(jnp.bfloat16)
    second = (values + batch_product(correction, first)).astype(jnp.bfloat16)
    return values.astype(jnp.float32) + batch_product(correction, second)


def reference(lower, upper, rhs):
    count = ROWS * LANES
    lower_blocks = lower.reshape(count, W, W).at[0].set(jnp.zeros((W, W), jnp.bfloat16))
    upper_blocks = upper.reshape(count, W, W).at[count - 1].set(jnp.zeros((W, W), jnp.bfloat16))
    right_side = rhs.reshape(count, W, K)
    correction = (batch_product(lower_blocks, from_below(upper_blocks, 1))
                  + batch_product(upper_blocks, from_above(lower_blocks, 1))).astype(jnp.bfloat16)
    lower_terms = (-batch_product(lower_blocks, from_below(lower_blocks, 1))).astype(jnp.bfloat16)
    upper_terms = (-batch_product(upper_blocks, from_above(upper_blocks, 1))).astype(jnp.bfloat16)
    source = (right_side.astype(jnp.float32) - batch_product(lower_blocks, from_below(right_side, 1))
              - batch_product(upper_blocks, from_above(right_side, 1))).astype(jnp.bfloat16)
    lower_one = horner(correction, lower_terms).astype(jnp.bfloat16)
    upper_one = horner(correction, upper_terms).astype(jnp.bfloat16)
    right_one = horner(correction, source).astype(jnp.bfloat16)
    correction_two = (batch_product(lower_one, from_below(upper_one, 2))
                      + batch_product(upper_one, from_above(lower_one, 2))).astype(jnp.bfloat16)
    source_two = (right_one.astype(jnp.float32) - batch_product(lower_one, from_below(right_one, 2))
                  - batch_product(upper_one, from_above(right_one, 2))).astype(jnp.bfloat16)
    result = horner(correction_two, source_two)
    return result.reshape(ROWS, LANES, W, K)
```

```python
import jax
import jax.numpy as jnp
from jax import lax
from jax.experimental import pallas as pl
from jax.experimental.pallas import tpu as pltpu
from jax.sharding import PartitionSpec as P

MESH = pl.DeviceIdType.MESH
W = 512
PIECES = 4
PIECE = W // PIECES
L, U, F = 0, 1, 2
FIRST_COLUMNS = ((0, 256), (256, 256))
LAST_COLUMNS = ((0, 256), (256, 128), (384, 128))


def dot(left, right):
    return jnp.dot(left, right, preferred_element_type=jnp.float32)


def device_at(x, y, z, core):
    return (z * 4 + y // 2 * 2 + core, y % 2 * 4 + x)


def chip_of_row(row):
    return row % 8 // 2, row % 2 * 2 + 1 - row // 8


def piece(ref, kind, index):
    span = pl.ds(index * PIECE, PIECE)
    return ref.at[:, span] if kind == F else ref.at[span]


def kernel(
    lower, upper, rhs, out,
    own, near, corr, terms, inner, one, far, result,
    in_send, in_recv, core_send, halo_send, near_recv,
    far_send, far_recv, out_send, out_recv,
):
    cuts, col = lax.axis_index("cuts"), lax.axis_index("col")
    x, z, core = col % 4, cuts // 4, cuts % 2
    half = cuts // 2 % 2
    y = half * 2 + col // 4
    parity = 1 - y % 2
    row = parity * 8 + x * 2 + half
    next_x, next_y = chip_of_row((row + 1) % 16)
    prev_x, prev_y = chip_of_row((row + 15) % 16)
    end, start = z == 7, z == 0
    next_x, next_y = jnp.where(end, next_x, x), jnp.where(end, next_y, y)
    prev_x, prev_y = jnp.where(start, prev_x, x), jnp.where(start, prev_y, y)
    next_z, prev_z = (z + 1) % 8, (z + 7) % 8

    sides = [device_at(x, 2 * side + parity, z, core) for side in (0, 1)]
    twin = device_at(x, y, z, 1 - core)
    following = device_at(next_x, next_y, next_z, core)
    preceding = device_at(prev_x, prev_y, prev_z, core)
    upward = core == 1
    halo = device_at(
        jnp.where(upward, next_x, prev_x),
        jnp.where(upward, next_y, prev_y),
        jnp.where(upward, next_z, prev_z),
        1 - core,
    )

    barrier = pltpu.get_barrier_semaphore()
    for partner in (*sides, twin, following, preceding, halo):
        pl.semaphore_signal(barrier, inc=1, device_id=partner, device_id_type=MESH)
    pl.semaphore_wait(barrier, 6)

    sent = []

    def send(source, target, send_sem, recv_sem, device):
        copy = pltpu.make_async_remote_copy(
            src_ref=source,
            dst_ref=target,
            send_sem=send_sem,
            recv_sem=recv_sem,
            device_id=device,
            device_id_type=MESH,
        )
        copy.start()
        sent.append(copy)

    def arrive(target, recv_sem):
        pltpu.make_async_remote_copy(
            src_ref=target,
            dst_ref=target,
            send_sem=recv_sem,
            recv_sem=recv_sem,
            device_id=twin,
            device_id_type=MESH,
        ).wait_recv()

    for kind, source in ((L, lower), (U, upper), (F, rhs)):
        for index in range(PIECES):
            for side in (0, 1):
                send(
                    piece(source.at[side], kind, index),
                    piece(own.at[half, kind], kind, index),
                    in_send.at[side, kind, index],
                    in_recv.at[half, kind, index],
                    sides[side],
                )

    first_slice = (row == 0) & start & (core == 0)
    last_slice = (row == 15) & end & (core == 1)

    def forward(kind, index):
        for slot in (0, 1):
            part = piece(own.at[slot, kind], kind, index)
            arrive(part, in_recv.at[slot, kind, index])
            edge = {(0, L): first_slice, (1, U): last_slice}.get((slot, kind))
            if edge is not None:

                @pl.when(edge)
                def _(part=part):
                    part[...] = jnp.zeros(part.shape, part.dtype)

            send(
                part,
                piece(near.at[slot + core, kind], kind, index),
                core_send.at[slot, kind, index],
                near_recv.at[slot + core, kind, index],
                twin,
            )
        send(
            piece(own.at[core, kind], kind, index),
            piece(near.at[2 - 2 * core, kind], kind, index),
            halo_send.at[kind, index],
            near_recv.at[2 - 2 * core, kind, index],
            halo,
        )

    def settle(kind, index):
        for slot in range(3):
            arrive(piece(near.at[slot, kind], kind, index), near_recv.at[slot, kind, index])

    def horner(matrix, values, columns, store):
        span = pl.ds(*columns)
        wide = lambda: values[:, span].astype(jnp.float32)
        inner[0, :, span] = (wide() + dot(matrix[...], values[:, span])).astype(jnp.bfloat16)
        inner[1, :, span] = (wide() + dot(matrix[...], inner[0, :, span])).astype(jnp.bfloat16)
        store[:, span] = (wide() + dot(matrix[...], inner[1, :, span])).astype(jnp.bfloat16)

    whole = (0, W)

    def correct(slot):
        corr[slot] = (
            dot(own[slot, L], near[slot, U]) + dot(own[slot, U], near[slot + 1, L])
        ).astype(jnp.bfloat16)

    def couple(slot, kind):
        other = near.at[slot + kind, kind]
        terms[slot, kind] = (-dot(own[slot, kind], other[...])).astype(jnp.bfloat16)

    def reduce_block(slot, kind):
        horner(corr.at[slot], terms.at[slot, kind], whole, one.at[slot, kind])

    def reduce_right(columns):
        span = pl.ds(*columns)
        for slot in (0, 1):
            terms[slot, F, :, span] = (
                own[slot, F, :, span].astype(jnp.float32)
                - dot(own[slot, L], near[slot, F, :, span])
                - dot(own[slot, U], near[slot + 1, F, :, span])
            ).astype(jnp.bfloat16)
            horner(corr.at[slot], terms.at[slot, F], columns, one.at[slot, F])

    def send_block(slot, kind, device):
        send(
            one.at[slot, kind],
            far.at[1 - slot, 0],
            far_send.at[1 - slot, PIECES],
            far_recv.at[1 - slot, PIECES],
            device,
        )

    def send_right(index):
        for slot, device in ((0, preceding), (1, following)):
            send(
                piece(one.at[slot, F], F, index),
                piece(far.at[1 - slot, 1], F, index),
                far_send.at[1 - slot, index],
                far_recv.at[1 - slot, index],
                device,
            )

    for index in range(PIECES):
        forward(L, index)
    for index in range(PIECES):
        settle(L, index)
    couple(0, L)
    couple(1, L)
    for index in range(PIECES):
        forward(U, index)
    for index in range(PIECES):
        settle(U, index)
    correct(0)
    reduce_block(0, L)
    send_block(0, L, preceding)
    correct(1)
    couple(1, U)
    reduce_block(1, U)
    send_block(1, U, following)
    forward(F, 0)
    couple(0, U)
    reduce_block(0, U)
    reduce_block(1, L)
    forward(F, 1)
    forward(F, 2)
    settle(F, 0)
    settle(F, 1)
    reduce_right(FIRST_COLUMNS[0])
    send_right(0)
    send_right(1)
    forward(F, 3)
    settle(F, 2)
    settle(F, 3)
    reduce_right(FIRST_COLUMNS[1])
    send_right(2)
    send_right(3)

    for side in (0, 1):
        arrive(far.at[side, 0], far_recv.at[side, PIECES])
    corr[0] = (dot(one[0, L], far[0, 0]) + dot(one[0, U], one[1, L])).astype(jnp.bfloat16)
    corr[1] = (dot(one[1, L], one[0, U]) + dot(one[1, U], far[1, 0])).astype(jnp.bfloat16)
    for columns in LAST_COLUMNS:
        span = pl.ds(*columns)
        indices = range(columns[0] // PIECE, (columns[0] + columns[1]) // PIECE)
        for index in indices:
            for side in (0, 1):
                arrive(piece(far.at[side, 1], F, index), far_recv.at[side, index])
        below = (far.at[0, 1], one.at[0, F])
        above = (one.at[1, F], far.at[1, 1])
        for slot in (0, 1):
            terms[slot, F, :, span] = (
                one[slot, F, :, span].astype(jnp.float32)
                - dot(one[slot, L], below[slot][:, span])
                - dot(one[slot, U], above[slot][:, span])
            ).astype(jnp.bfloat16)
            horner(corr.at[slot], terms.at[slot, F], columns, result.at[slot])
            for index in indices:
                send(
                    piece(result.at[slot], F, index),
                    piece(out.at[half], F, index),
                    out_send.at[slot, index],
                    out_recv.at[half, index],
                    sides[slot],
                )
    for index in range(PIECES):
        for side in (0, 1):
            arrive(piece(out.at[side], F, index), out_recv.at[side, index])
    for copy in sent:
        copy.wait_send()


def on_device(lower, upper, rhs):
    blocks = lambda *lead: pltpu.VMEM((*lead, W, W), jnp.bfloat16)
    copies = lambda *lead: pltpu.SemaphoreType.DMA(lead)
    hbm = pl.BlockSpec(memory_space=pl.ANY)
    reduced = pl.pallas_call(
        kernel,
        out_shape=jax.ShapeDtypeStruct((2, W, W), jnp.bfloat16),
        in_specs=[hbm] * 3,
        out_specs=hbm,
        scratch_shapes=[
            blocks(2, 3),
            blocks(3, 3),
            blocks(2),
            blocks(2, 3),
            blocks(2),
            blocks(2, 3),
            blocks(2, 2),
            blocks(2),
            copies(2, 3, PIECES),
            copies(2, 3, PIECES),
            copies(2, 3, PIECES),
            copies(3, PIECES),
            copies(3, 3, PIECES),
            copies(2, PIECES + 1),
            copies(2, PIECES + 1),
            copies(2, PIECES),
            copies(2, PIECES),
        ],
        compiler_params=pltpu.CompilerParams(
            collective_id=0, has_side_effects=True, vmem_limit_bytes=48 * 2**20
        ),
    )(lower[:, 0], upper[:, 0], rhs[:, 0])
    return reduced.astype(jnp.float32)[:, None]


def solution(mesh):
    return jax.shard_map(
        on_device,
        mesh=mesh,
        in_specs=(P("col", "cuts", None, None),) * 3,
        out_specs=P("col", "cuts", None, None),
        check_vma=False,
    )
```

```python
import jax
import jax.numpy as jnp
from jax import lax
from jax.experimental import pallas as pl
from jax.experimental.pallas import tpu as pltpu
from jax.sharding import PartitionSpec as P

MESH = pl.DeviceIdType.MESH
W = 512
PIECES = 4
PIECE = W // PIECES
RELAYED = (3,)
L, U, F = 0, 1, 2
COLUMNS = ((0, 256), (256, 256))


def dot(left, right):
    return jnp.dot(left, right, preferred_element_type=jnp.float32)


def device_at(x, y, z, core):
    return (z * 4 + y // 2 * 2 + core, y % 2 * 4 + x)


def chip_of_row(row):
    return row % 8 // 2, row % 2 * 2 + row // 8


def piece(ref, kind, index):
    span = pl.ds(index * PIECE, PIECE)
    return ref.at[:, span] if kind == F else ref.at[span]


def choose(condition, first, second):
    return tuple(jnp.where(condition, one, other) for one, other in zip(first, second))


def flip(chip):
    return chip[0], (chip[1] + 2) % 4


def kernel(
    lower, upper, rhs, out,
    mine, near, relay, corr, left_terms, right_terms, sources, left_one, right_one, fields, inner, result,
    keep_sem, in_send, relay_send, relay_recv, extra_send, mine_recv, near_recv,
    twin_send, chain_send, cross_send, halo_send, out_send, out_recv,
):
    cuts, col = lax.axis_index("cuts"), lax.axis_index("col")
    x, low, z, core = col % 4, col // 4, cuts // 4, cuts % 2
    half = cuts // 2 % 2
    y = half * 2 + low
    row = low * 8 + x * 2 + half
    top, bottom = z == 7, z == 0
    first, second = half == 0, half == 1
    lead = (top & second) | (bottom & first)
    trail = (top & first) | (bottom & second)

    next_z, prev_z = (z + 1) % 8, (z + 7) % 8
    next_chip = choose(top, chip_of_row((row + 1) % 16), (x, y))
    prev_chip = choose(bottom, chip_of_row((row + 15) % 16), (x, y))
    has_next, has_prev = ~(top & (row == 15)), ~(bottom & (row == 0))
    partner = device_at(x, (y + 2) % 4, z, core)
    twin = device_at(x, y, z, 1 - core)
    following, following_cross = (device_at(*next_chip, next_z, c) for c in (core, 1 - core))
    preceding, preceding_cross = (device_at(*prev_chip, prev_z, c) for c in (core, 1 - core))

    end = top | bottom
    end_z = jnp.where(top, 0, 7)
    end_chip = choose(top, next_chip, prev_chip)
    has_end = jnp.where(top, has_next, has_prev) & end
    partner_row = row + 1 - 2 * half
    step = jnp.where(top, 1, 15)
    partner_end = chip_of_row((partner_row + step) % 16)
    partner_has_end = end & ~(top & (partner_row == 15)) & ~(bottom & (partner_row == 0))
    goal, goal_cross = (device_at(*partner_end, end_z, c) for c in (core, 1 - core))
    origin, origin_cross = (device_at(*flip(end_chip), end_z, c) for c in (core, 1 - core))
    chain_end, chain_end_cross = (device_at(*end_chip, end_z, c) for c in (core, 1 - core))
    crosses = (top & (core == 1)) | (bottom & (core == 0))

    def copy_in(kind, source):
        return pltpu.make_async_copy(source.at[half], mine.at[1 + half, kind], keep_sem.at[kind])

    kinds = ((L, lower), (U, upper), (F, rhs))
    for kind, source in kinds:
        copy_in(kind, source).start()

    barrier = pltpu.get_barrier_semaphore()

    def greet(device, condition):
        @pl.when(condition)
        def _():
            pl.semaphore_signal(barrier, inc=1, device_id=device, device_id_type=MESH)

    greet(partner, core < 2)
    greet(twin, core < 2)
    greet(following, ~top)
    greet(preceding, ~bottom)
    greet(following_cross, ~top & (core == 1))
    greet(preceding_cross, ~bottom & (core == 0))
    greet(chain_end, has_end & lead)
    greet(origin, has_end)
    greet(origin_cross, has_end & lead & crosses)
    greet(chain_end_cross, has_end & trail & crosses)
    expected = (
        ~top,
        ~bottom,
        ~top & (core == 1),
        ~bottom & (core == 0),
        has_end & lead,
        partner_has_end,
        partner_has_end & trail & crosses,
        has_end & trail & crosses,
    )
    pl.semaphore_wait(barrier, 2 + sum(flag.astype(jnp.int32) for flag in expected))

    sent = []

    def only(condition, action):
        if condition is None:
            action()
        else:
            pl.when(condition)(action)

    gate = [None]

    def gated(condition):
        if gate[0] is None:
            return condition
        return gate[0] if condition is None else gate[0] & condition

    def send(source, target, send_sem, recv_sem, device, condition=None):
        condition = gated(condition)
        copy = pltpu.make_async_remote_copy(
            src_ref=source,
            dst_ref=target,
            send_sem=send_sem,
            recv_sem=recv_sem,
            device_id=device,
            device_id_type=MESH,
        )
        only(condition, copy.start)
        sent.append((condition, copy))

    def arrive(target, recv_sem, condition=None):
        condition = gated(condition)
        copy = pltpu.make_async_remote_copy(
            src_ref=target,
            dst_ref=target,
            send_sem=recv_sem,
            recv_sem=recv_sem,
            device_id=twin,
            device_id_type=MESH,
        )
        only(condition, copy.wait_recv)

    def to_mine(source, slot, kind, index, send_sem, device, condition):
        send(
            source,
            piece(mine.at[slot, kind], kind, index),
            send_sem,
            mine_recv.at[slot, kind, index],
            device,
            condition,
        )

    def to_near(source, slot, kind, index, send_sem, device, condition=None):
        send(
            source,
            piece(near.at[slot, kind], kind, index),
            send_sem,
            near_recv.at[slot, kind, index],
            device,
            condition,
        )

    mine_end = jnp.where(top, 0, 3)
    near_end = jnp.where(top, 0, 4)

    def reaches(kind, upward):
        return kind == F or (kind == U) == upward

    for kind, source in kinds:
        for index in range(PIECES):
            other = piece(source.at[1 - half], kind, index)
            to_mine(other, 1 + half, kind, index, in_send.at[kind, index], partner, None)
            to_mine(other, mine_end, kind, index, extra_send.at[0, kind, index], goal, lead)
            if index in RELAYED:
                send(
                    piece(source.at[half], kind, index),
                    piece(relay.at[kind], kind, index),
                    relay_send.at[0, kind, index],
                    relay_recv.at[kind, index],
                    partner,
                    lead & has_end,
                )
            for upward, side in ((True, top), (False, bottom)):
                if reaches(kind, upward):
                    to_near(
                        other,
                        0 if upward else 4,
                        kind,
                        index,
                        extra_send.at[1 if upward else 2, kind, index],
                        goal_cross,
                        trail & partner_has_end & crosses & side,
                    )

    first_slice = (row == 0) & bottom & (core == 0)
    last_slice = (row == 15) & top & (core == 1)

    def blank(ref, condition):
        condition = gated(condition)

        @pl.when(condition)
        def _():
            ref[...] = jnp.zeros(ref.shape, ref.dtype)

    blank(mine.at[0], ~has_prev)
    blank(mine.at[3], ~has_next)
    blank(near.at[0], ~has_prev & (core == 0))
    blank(near.at[4], ~has_next & (core == 1))

    def cut(slot, kind, part):
        if kind != F:
            blank(part, (first_slice & (slot == 1)) if kind == L else (last_slice & (slot == 2)))

    def pass_on(slot, kind, index, local):
        part = piece(mine.at[slot, kind], kind, index)
        number = 0 if local else 1
        to_near(part, slot + core, kind, index, twin_send.at[number, kind, index], twin)
        upward = second if local else first
        if local:
            chain = ~lead if index in RELAYED else None
        else:
            chain = ~trail
        for way, device, there, target in (
            (upward, following, has_next, 0),
            (~upward, preceding, has_prev, 3),
        ):
            condition = way & there if chain is None else way & there & chain
            to_mine(part, target, kind, index, chain_send.at[number, target // 3, kind, index], device, condition)
        cross = (core != half) if local else (core == half) & ~lead
        for way, device, there, target in (
            (core == 1, following_cross, has_next, 0),
            (core == 0, preceding_cross, has_prev, 4),
        ):
            if reaches(kind, target == 0):
                to_near(
                    part,
                    target,
                    kind,
                    index,
                    cross_send.at[number, target // 4, kind, index],
                    device,
                    way & there & cross,
                )

    def local(kind):
        copy_in(kind, kinds[kind][1]).wait()
        cut(1 + half, kind, mine.at[1 + half, kind])
        for index in range(PIECES):
            pass_on(1 + half, kind, index, True)

    def forward(kind, index):
        part = piece(mine.at[2 - half, kind], kind, index)
        arrive(part, mine_recv.at[2 - half, kind, index])
        cut(2 - half, kind, part)
        pass_on(2 - half, kind, index, False)
        if index in RELAYED:
            part = piece(relay.at[kind], kind, index)
            waiting = trail & partner_has_end
            arrive(part, relay_recv.at[kind, index], waiting)
            to_mine(part, mine_end, kind, index, relay_send.at[1, kind, index], goal, waiting)

    def halo(kind, index):
        for slot, there in ((0, has_prev), (3, has_next)):
            part = piece(mine.at[slot, kind], kind, index)
            arrive(part, mine_recv.at[slot, kind, index], there)
            upward = slot == 0
            condition = None if reaches(kind, upward) else (core == 1) if upward else (core == 0)
            to_near(
                part, slot + core, kind, index, halo_send.at[slot // 3, kind, index], twin, condition
            )

    def settle(slot, kind, index):
        if slot in (0, 4) and not reaches(kind, slot == 0):
            return
        condition = {0: (core == 1) | has_prev, 4: (core == 0) | has_next}.get(slot)
        arrive(piece(near.at[slot, kind], kind, index), near_recv.at[slot, kind, index], condition)

    def settle_blocks(*slots):
        for slot in slots:
            for kind in (L, U):
                for index in range(PIECES):
                    settle(slot, kind, index)

    def horner(jobs):
        for step in range(3):
            for number, (matrix, values, store) in enumerate(jobs):
                width = values.shape[1]
                last = values if step == 0 else inner.at[number, step - 1, :, pl.ds(0, width)]
                target = store if step == 2 else inner.at[number, step, :, pl.ds(0, width)]
                target[...] = (values[...].astype(jnp.float32) + dot(matrix[...], last[...])).astype(
                    jnp.bfloat16
                )

    def correct(k):
        corr[k] = (dot(mine[k, L], near[k, U]) + dot(mine[k, U], near[k + 1, L])).astype(jnp.bfloat16)

    def couple_left(k):
        left_terms[k] = (-dot(mine[k, L], near[k, L])).astype(jnp.bfloat16)
        return corr.at[k], left_terms.at[k], left_one.at[k]

    def couple_right(k):
        right_terms[k] = (-dot(mine[k, U], near[k + 1, U])).astype(jnp.bfloat16)
        return corr.at[k], right_terms.at[k], right_one.at[k]

    def source(values, left, right, before, after, span):
        return (
            values[:, span].astype(jnp.float32)
            - dot(left[...], before[:, span])
            - dot(right[...], after[:, span])
        ).astype(jnp.bfloat16)

    def forward_if(condition, index):
        gate[0] = condition
        forward(F, index)
        gate[0] = None

    def settle_if(condition, *slots):
        gate[0] = condition
        settle_blocks(*slots)
        gate[0] = None

    every = range(PIECES)
    inside = ~end
    local(L)
    local(U)
    for kind in (L, U):
        for index in every:
            forward(kind, index)
    local(F)
    for index in every:
        halo(L, index)
    settle_blocks(2)
    settle_if(core == 0, 3)
    settle_if(core == 1, 1)
    k = 2 - core
    correct(k)
    horner([couple_left(k), couple_right(k)])
    forward_if(inside, 0)
    forward_if(inside, 1)
    for index in every:
        halo(U, index)
    forward_if(end, 0)
    settle_if(core == 0, 1)
    settle_if(core == 1, 3)
    k = 1 + core
    correct(k)
    horner([couple_left(k), couple_right(k)])
    forward_if(inside, 2)
    forward_if(end, 1)
    settle_blocks(0, 4)
    correct(0)
    correct(3)
    horner([couple_right(0), couple_left(3)])
    forward_if(inside, 3)
    forward_if(end, 2)

    for k in (1, 2):
        corr[3 + k] = (
            dot(left_one[k], right_one[k - 1]) + dot(right_one[k], left_one[k + 1])
        ).astype(jnp.bfloat16)

    def home_copy(slot, index):
        return pltpu.make_async_copy(
            piece(result.at[slot], F, index), piece(out.at[half], F, index), keep_sem.at[3 + index]
        )

    def send_out(slot, index):
        pl.when(half == slot)(home_copy(slot, index).start)
        send(
            piece(result.at[slot], F, index),
            piece(out.at[half], F, index),
            out_send.at[index],
            out_recv.at[index],
            partner,
            half != slot,
        )

    for columns in COLUMNS:
        span = pl.ds(*columns)
        indices = range(columns[0] // PIECE, (columns[0] + columns[1]) // PIECE)
        for index in indices:
            halo(F, index)
        if columns[0] == 0:
            forward_if(end, 3)
        for index in indices:
            for slot in range(5):
                settle(slot, F, index)
        jobs = []
        for k in range(4):
            sources[k, :, span] = source(
                mine.at[k, F], mine.at[k, L], mine.at[k, U], near.at[k, F], near.at[k + 1, F], span
            )
            jobs.append((corr.at[k], sources.at[k, :, span], fields.at[k, :, span]))
        horner(jobs)
        jobs = []
        for slot in (0, 1):
            k = slot + 1
            sources[k, :, span] = source(
                fields.at[k], left_one.at[k], right_one.at[k], fields.at[k - 1], fields.at[k + 1], span
            )
            jobs.append((corr.at[3 + k], sources.at[k, :, span], result.at[slot, :, span]))
        horner(jobs)
        for slot in (0, 1):
            for index in indices:
                send_out(slot, index)
    for index in range(PIECES):
        for slot in (0, 1):
            pl.when(half == slot)(home_copy(slot, index).wait)
        arrive(piece(out.at[1 - half], F, index), out_recv.at[index])
    for condition, copy in sent:
        only(condition, copy.wait_send)


def on_device(lower, upper, rhs):
    blocks = lambda *lead: pltpu.VMEM((*lead, W, W), jnp.bfloat16)
    copies = lambda *lead: pltpu.SemaphoreType.DMA(lead)
    hbm = pl.BlockSpec(memory_space=pltpu.HBM)
    reduced = pl.pallas_call(
        kernel,
        out_shape=jax.ShapeDtypeStruct((2, W, W), jnp.bfloat16),
        in_specs=[hbm] * 3,
        out_specs=pl.BlockSpec(memory_space=pl.ANY),
        scratch_shapes=[
            blocks(4, 3),
            blocks(5, 3),
            blocks(3),
            blocks(6),
            blocks(4),
            blocks(4),
            blocks(4),
            blocks(4),
            blocks(4),
            blocks(4),
            blocks(4, 2),
            blocks(2),
            copies(3 + PIECES),
            copies(3, PIECES),
            copies(2, 3, PIECES),
            copies(3, PIECES),
            copies(3, 3, PIECES),
            copies(4, 3, PIECES),
            copies(5, 3, PIECES),
            copies(2, 3, PIECES),
            copies(2, 2, 3, PIECES),
            copies(2, 2, 3, PIECES),
            copies(2, 3, PIECES),
            copies(PIECES),
            copies(PIECES),
        ],
        compiler_params=pltpu.CompilerParams(
            collective_id=0, has_side_effects=True, vmem_limit_bytes=60 * 2**20
        ),
    )(lower[:, 0], upper[:, 0], rhs[:, 0])
    return reduced.astype(jnp.float32)[:, None]


def solution(mesh):
    return jax.shard_map(
        on_device,
        mesh=mesh,
        in_specs=(P("col", "cuts", None, None),) * 3,
        out_specs=P("col", "cuts", None, None),
        check_vma=False,
    )
```

```python
import jax
import jax.numpy as jnp
from jax import lax
from jax.experimental import pallas as pl
from jax.experimental.pallas import tpu as pltpu
from jax.sharding import PartitionSpec as P

MESH = pl.DeviceIdType.MESH
W = 512
PIECES = 4
PIECE = W // PIECES
RELAYED = ((0, 3), (1, 2), (1, 3))
BENT = (*RELAYED, (0, 2))
L, U, F = 0, 1, 2
COLUMNS = ((0, 256), (256, 256))


def dot(left, right):
    return jnp.dot(left, right, preferred_element_type=jnp.float32)


def device_at(x, y, z, core):
    return (z * 4 + y // 2 * 2 + core, y % 2 * 4 + x)


def chip_of_row(row):
    return row % 8 // 2, row % 2 * 2 + row // 8


def piece(ref, kind, index):
    span = pl.ds(index * PIECE, PIECE)
    return ref.at[:, span] if kind == F else ref.at[span]


def choose(condition, first, second):
    return tuple(jnp.where(condition, one, other) for one, other in zip(first, second))


def flip(chip):
    return chip[0], (chip[1] + 2) % 4


def kernel(
    lower, upper, rhs, out,
    mine, near, relay, corr, left_terms, right_terms, sources, left_one, right_one, fields, inner, result,
    keep_sem, in_send, relay_send, relay_recv, extra_send, mine_recv, near_recv,
    twin_send, chain_send, cross_send, halo_send, out_send, out_recv,
):
    cuts, col = lax.axis_index("cuts"), lax.axis_index("col")
    x, low, z, core = col % 4, col // 4, cuts // 4, cuts % 2
    half = cuts // 2 % 2
    y = half * 2 + low
    row = low * 8 + x * 2 + half
    top, bottom = z == 7, z == 0
    first, second = half == 0, half == 1
    lead = (top & second) | (bottom & first)
    trail = (top & first) | (bottom & second)

    next_z, prev_z = (z + 1) % 8, (z + 7) % 8
    next_chip = choose(top, chip_of_row((row + 1) % 16), (x, y))
    prev_chip = choose(bottom, chip_of_row((row + 15) % 16), (x, y))
    has_next, has_prev = ~(top & (row == 15)), ~(bottom & (row == 0))
    partner = device_at(x, (y + 2) % 4, z, core)
    twin = device_at(x, y, z, 1 - core)
    following, following_cross = (device_at(*next_chip, next_z, c) for c in (core, 1 - core))
    preceding, preceding_cross = (device_at(*prev_chip, prev_z, c) for c in (core, 1 - core))

    end = top | bottom
    end_z = jnp.where(top, 0, 7)
    end_chip = choose(top, next_chip, prev_chip)
    has_end = jnp.where(top, has_next, has_prev) & end
    partner_row = row + 1 - 2 * half
    step = jnp.where(top, 1, 15)
    partner_end = chip_of_row((partner_row + step) % 16)
    partner_has_end = end & ~(top & (partner_row == 15)) & ~(bottom & (partner_row == 0))
    goal, goal_cross = (device_at(*partner_end, end_z, c) for c in (core, 1 - core))
    origin, origin_cross = (device_at(*flip(end_chip), end_z, c) for c in (core, 1 - core))
    chain_end, chain_end_cross = (device_at(*end_chip, end_z, c) for c in (core, 1 - core))

    bend = (top & (row == 7)) | (bottom & (row == 8))
    partner_bend = (top & (partner_row == 7)) | (bottom & (partner_row == 8))
    bend_relay = (top & (row == 14)) | (bottom & (row == 1))
    relay_to = device_at(x, (y + jnp.where(bend, jnp.where(top, 3, 1), 2)) % 4, z, core)
    relay_goal = choose(bend_relay, chip_of_row(jnp.where(top, 8, 7)), partner_end)
    relay_goal = device_at(*relay_goal, end_z, core)
    bend_sender = device_at(*chip_of_row(jnp.where(top, 7, 8)), z, core)
    bend_source = device_at(*chip_of_row(jnp.where(top, 1, 14)), end_z, core)
    crosses = (top & (core == 1)) | (bottom & (core == 0))

    def copy_in(kind, source):
        return pltpu.make_async_copy(source.at[half], mine.at[1 + half, kind], keep_sem.at[kind])

    kinds = ((L, lower), (U, upper), (F, rhs))
    for kind, source in kinds:
        copy_in(kind, source).start()

    barrier = pltpu.get_barrier_semaphore()

    def greet(device, condition):
        @pl.when(condition)
        def _():
            pl.semaphore_signal(barrier, inc=1, device_id=device, device_id_type=MESH)

    greet(partner, core < 2)
    greet(twin, core < 2)
    greet(following, ~top)
    greet(preceding, ~bottom)
    greet(following_cross, ~top & (core == 1))
    greet(preceding_cross, ~bottom & (core == 0))
    greet(chain_end, has_end & lead)
    greet(origin, has_end)
    greet(bend_sender, bend_relay)
    greet(bend_source, bend)
    greet(origin_cross, has_end & lead & crosses)
    greet(chain_end_cross, has_end & trail & crosses)
    expected = (
        ~top,
        ~bottom,
        ~top & (core == 1),
        ~bottom & (core == 0),
        has_end & lead,
        bend,
        bend_relay,
        partner_has_end,
        partner_has_end & trail & crosses,
        has_end & trail & crosses,
    )
    pl.semaphore_wait(barrier, 2 + sum(flag.astype(jnp.int32) for flag in expected))

    sent = []

    def only(condition, action):
        if condition is None:
            action()
        else:
            pl.when(condition)(action)

    gate = [None]

    def gated(condition):
        if gate[0] is None:
            return condition
        return gate[0] if condition is None else gate[0] & condition

    def send(source, target, send_sem, recv_sem, device, condition=None):
        condition = gated(condition)
        copy = pltpu.make_async_remote_copy(
            src_ref=source,
            dst_ref=target,
            send_sem=send_sem,
            recv_sem=recv_sem,
            device_id=device,
            device_id_type=MESH,
        )
        only(condition, copy.start)
        sent.append((condition, copy))

    def arrive(target, recv_sem, condition=None):
        condition = gated(condition)
        copy = pltpu.make_async_remote_copy(
            src_ref=target,
            dst_ref=target,
            send_sem=recv_sem,
            recv_sem=recv_sem,
            device_id=twin,
            device_id_type=MESH,
        )
        only(condition, copy.wait_recv)

    def to_mine(source, slot, kind, index, send_sem, device, condition):
        send(
            source,
            piece(mine.at[slot, kind], kind, index),
            send_sem,
            mine_recv.at[slot, kind, index],
            device,
            condition,
        )

    def to_near(source, slot, kind, index, send_sem, device, condition=None):
        send(
            source,
            piece(near.at[slot, kind], kind, index),
            send_sem,
            near_recv.at[slot, kind, index],
            device,
            condition,
        )

    mine_end = jnp.where(top, 0, 3)
    near_end = jnp.where(top, 0, 4)

    def reaches(kind, upward):
        return kind == F or (kind == U) == upward

    def start(kind):
        source = kinds[kind][1]
        for index in range(PIECES):
            other = piece(source.at[1 - half], kind, index)
            to_mine(other, 1 + half, kind, index, in_send.at[kind, index], partner, None)
            to_mine(other, mine_end, kind, index, extra_send.at[0, kind, index], goal, lead)
            if (kind, index) in BENT:
                send(
                    piece(source.at[half], kind, index),
                    piece(relay.at[kind], kind, index),
                    relay_send.at[0, kind, index],
                    relay_recv.at[kind, index],
                    relay_to,
                    lead & has_end if (kind, index) in RELAYED else bend,
                )
            for upward, side in ((True, top), (False, bottom)):
                if reaches(kind, upward):
                    to_near(
                        other,
                        0 if upward else 4,
                        kind,
                        index,
                        extra_send.at[1 if upward else 2, kind, index],
                        goal_cross,
                        trail & partner_has_end & crosses & side,
                    )

    first_slice = (row == 0) & bottom & (core == 0)
    last_slice = (row == 15) & top & (core == 1)

    def blank(ref, condition):
        condition = gated(condition)

        @pl.when(condition)
        def _():
            ref[...] = jnp.zeros(ref.shape, ref.dtype)

    blank(mine.at[0], ~has_prev)
    blank(mine.at[3], ~has_next)
    blank(near.at[0], ~has_prev & (core == 0))
    blank(near.at[4], ~has_next & (core == 1))

    def cut(slot, kind, part):
        if kind != F:
            blank(part, (first_slice & (slot == 1)) if kind == L else (last_slice & (slot == 2)))

    def pass_on(slot, kind, index, local):
        part = piece(mine.at[slot, kind], kind, index)
        number = 0 if local else 1
        to_near(part, slot + core, kind, index, twin_send.at[number, kind, index], twin)
        upward = second if local else first
        if local:
            bent = ~bend if (kind, index) in BENT else None
            chain = ~lead if (kind, index) in RELAYED else bent
        else:
            chain = ~trail
        for way, device, there, target in (
            (upward, following, has_next, 0),
            (~upward, preceding, has_prev, 3),
        ):
            condition = way & there if chain is None else way & there & chain
            to_mine(part, target, kind, index, chain_send.at[number, target // 3, kind, index], device, condition)
        cross = (core != half) if local else (core == half) & ~lead
        for way, device, there, target in (
            (core == 1, following_cross, has_next, 0),
            (core == 0, preceding_cross, has_prev, 4),
        ):
            if reaches(kind, target == 0):
                to_near(
                    part,
                    target,
                    kind,
                    index,
                    cross_send.at[number, target // 4, kind, index],
                    device,
                    way & there & cross,
                )

    def local(kind):
        copy_in(kind, kinds[kind][1]).wait()
        cut(1 + half, kind, mine.at[1 + half, kind])
        for index in range(PIECES):
            pass_on(1 + half, kind, index, True)

    def forward(kind, index):
        part = piece(mine.at[2 - half, kind], kind, index)
        arrive(part, mine_recv.at[2 - half, kind, index])
        cut(2 - half, kind, part)
        pass_on(2 - half, kind, index, False)
        if (kind, index) in BENT:
            part = piece(relay.at[kind], kind, index)
            waiting = bend_relay
            if (kind, index) in RELAYED:
                waiting |= trail & partner_has_end & ~partner_bend
            arrive(part, relay_recv.at[kind, index], waiting)
            to_mine(part, mine_end, kind, index, relay_send.at[1, kind, index], relay_goal, waiting)

    def halo(kind, index):
        for slot, there in ((0, has_prev), (3, has_next)):
            part = piece(mine.at[slot, kind], kind, index)
            arrive(part, mine_recv.at[slot, kind, index], there)
            upward = slot == 0
            condition = None if reaches(kind, upward) else (core == 1) if upward else (core == 0)
            to_near(
                part, slot + core, kind, index, halo_send.at[slot // 3, kind, index], twin, condition
            )

    def settle(slot, kind, index):
        if slot in (0, 4) and not reaches(kind, slot == 0):
            return
        condition = {0: (core == 1) | has_prev, 4: (core == 0) | has_next}.get(slot)
        arrive(piece(near.at[slot, kind], kind, index), near_recv.at[slot, kind, index], condition)

    def settle_blocks(*slots):
        for slot in slots:
            for kind in (L, U):
                for index in range(PIECES):
                    settle(slot, kind, index)

    def horner(jobs):
        for step in range(3):
            for number, (matrix, values, store) in enumerate(jobs):
                width = values.shape[1]
                last = values if step == 0 else inner.at[number, step - 1, :, pl.ds(0, width)]
                target = store if step == 2 else inner.at[number, step, :, pl.ds(0, width)]
                target[...] = (values[...].astype(jnp.float32) + dot(matrix[...], last[...])).astype(
                    jnp.bfloat16
                )

    def correct(k):
        corr[k] = (dot(mine[k, L], near[k, U]) + dot(mine[k, U], near[k + 1, L])).astype(jnp.bfloat16)

    def couple_left(k):
        left_terms[k] = (-dot(mine[k, L], near[k, L])).astype(jnp.bfloat16)
        return corr.at[k], left_terms.at[k], left_one.at[k]

    def couple_right(k):
        right_terms[k] = (-dot(mine[k, U], near[k + 1, U])).astype(jnp.bfloat16)
        return corr.at[k], right_terms.at[k], right_one.at[k]

    def source(values, left, right, before, after, span):
        return (
            values[:, span].astype(jnp.float32)
            - dot(left[...], before[:, span])
            - dot(right[...], after[:, span])
        ).astype(jnp.bfloat16)

    def forward_if(condition, index):
        gate[0] = condition
        forward(F, index)
        gate[0] = None

    def settle_if(condition, *slots):
        gate[0] = condition
        settle_blocks(*slots)
        gate[0] = None

    every = range(PIECES)
    inside = ~end
    start(L)
    local(L)
    start(U)
    local(U)
    start(F)
    for kind in (L, U):
        for index in every:
            forward(kind, index)
    local(F)
    for index in every:
        halo(L, index)
    settle_blocks(2)
    settle_if(core == 0, 3)
    settle_if(core == 1, 1)
    k = 2 - core
    correct(k)
    horner([couple_left(k), couple_right(k)])
    forward_if(inside, 0)
    forward_if(inside, 1)
    for index in every:
        halo(U, index)
    forward_if(end, 0)
    settle_if(core == 0, 1)
    settle_if(core == 1, 3)
    k = 1 + core
    correct(k)
    horner([couple_left(k), couple_right(k)])
    forward_if(inside, 2)
    forward_if(end, 1)
    settle_blocks(0, 4)
    correct(0)
    correct(3)
    horner([couple_right(0), couple_left(3)])
    forward_if(inside, 3)
    forward_if(end, 2)

    for k in (1, 2):
        corr[3 + k] = (
            dot(left_one[k], right_one[k - 1]) + dot(right_one[k], left_one[k + 1])
        ).astype(jnp.bfloat16)

    def home_copy(slot, index):
        return pltpu.make_async_copy(
            piece(result.at[slot], F, index), piece(out.at[half], F, index), keep_sem.at[3 + index]
        )

    def send_out(slot, index):
        pl.when(half == slot)(home_copy(slot, index).start)
        send(
            piece(result.at[slot], F, index),
            piece(out.at[half], F, index),
            out_send.at[index],
            out_recv.at[index],
            partner,
            half != slot,
        )

    for columns in COLUMNS:
        span = pl.ds(*columns)
        indices = range(columns[0] // PIECE, (columns[0] + columns[1]) // PIECE)
        for index in indices:
            halo(F, index)
        if columns[0] == 0:
            forward_if(end, 3)
        for index in indices:
            for slot in range(5):
                settle(slot, F, index)
        jobs = []
        for k in range(4):
            sources[k, :, span] = source(
                mine.at[k, F], mine.at[k, L], mine.at[k, U], near.at[k, F], near.at[k + 1, F], span
            )
            jobs.append((corr.at[k], sources.at[k, :, span], fields.at[k, :, span]))
        horner(jobs)
        jobs = []
        for slot in (0, 1):
            k = slot + 1
            sources[k, :, span] = source(
                fields.at[k], left_one.at[k], right_one.at[k], fields.at[k - 1], fields.at[k + 1], span
            )
            jobs.append((corr.at[3 + k], sources.at[k, :, span], result.at[slot, :, span]))
        horner(jobs)
        for slot in (0, 1):
            for index in indices:
                send_out(slot, index)
    for index in range(PIECES):
        for slot in (0, 1):
            pl.when(half == slot)(home_copy(slot, index).wait)
        arrive(piece(out.at[1 - half], F, index), out_recv.at[index])
    for condition, copy in sent:
        only(condition, copy.wait_send)


def on_device(lower, upper, rhs):
    blocks = lambda *lead: pltpu.VMEM((*lead, W, W), jnp.bfloat16)
    copies = lambda *lead: pltpu.SemaphoreType.DMA(lead)
    hbm = pl.BlockSpec(memory_space=pltpu.HBM)
    reduced = pl.pallas_call(
        kernel,
        out_shape=jax.ShapeDtypeStruct((2, W, W), jnp.bfloat16),
        in_specs=[hbm] * 3,
        out_specs=pl.BlockSpec(memory_space=pl.ANY),
        scratch_shapes=[
            blocks(4, 3),
            blocks(5, 3),
            blocks(3),
            blocks(6),
            blocks(4),
            blocks(4),
            blocks(4),
            blocks(4),
            blocks(4),
            blocks(4),
            blocks(4, 2),
            blocks(2),
            copies(3 + PIECES),
            copies(3, PIECES),
            copies(2, 3, PIECES),
            copies(3, PIECES),
            copies(3, 3, PIECES),
            copies(4, 3, PIECES),
            copies(5, 3, PIECES),
            copies(2, 3, PIECES),
            copies(2, 2, 3, PIECES),
            copies(2, 2, 3, PIECES),
            copies(2, 3, PIECES),
            copies(PIECES),
            copies(PIECES),
        ],
        compiler_params=pltpu.CompilerParams(
            collective_id=0, has_side_effects=True, vmem_limit_bytes=60 * 2**20
        ),
    )(lower[:, 0], upper[:, 0], rhs[:, 0])
    return reduced.astype(jnp.float32)[:, None]


def solution(mesh):
    return jax.shard_map(
        on_device,
        mesh=mesh,
        in_specs=(P("col", "cuts", None, None),) * 3,
        out_specs=P("col", "cuts", None, None),
        check_vma=False,
    )
```

```python
import jax
import jax.numpy as jnp
from jax import lax
from jax.experimental import pallas as pl
from jax.experimental.pallas import tpu as pltpu
from jax.sharding import PartitionSpec as P

MESH = pl.DeviceIdType.MESH
W = 512
PIECES = 4
PIECE = W // PIECES
RELAYED = ((0, 3), (1, 2), (1, 3))
BENT = (*RELAYED, (0, 2))
L, U, F = 0, 1, 2
COLUMNS = ((0, 256), (256, 256))


def dot(left, right):
    return jnp.dot(left, right, preferred_element_type=jnp.float32)


def device_at(x, y, z, core):
    return (z * 4 + y // 2 * 2 + core, y % 2 * 4 + x)


def chip_of_row(row):
    return row % 8 // 2, row % 2 * 2 + row // 8


def piece(ref, kind, index):
    span = pl.ds(index * PIECE, PIECE)
    return ref.at[:, span] if kind == F else ref.at[span]


def choose(condition, first, second):
    return tuple(jnp.where(condition, one, other) for one, other in zip(first, second))


def flip(chip):
    return chip[0], (chip[1] + 2) % 4


def kernel(
    lower, upper, rhs, out,
    mine, near, relay, corr, left_terms, right_terms, sources, left_one, right_one, fields, inner, result,
    keep_sem, in_send, relay_send, relay_recv, extra_send, mine_recv, near_recv,
    twin_send, chain_send, cross_send, halo_send, out_send, out_recv,
):
    cuts, col = lax.axis_index("cuts"), lax.axis_index("col")
    x, low, z, core = col % 4, col // 4, cuts // 4, cuts % 2
    half = cuts // 2 % 2
    y = half * 2 + low
    row = low * 8 + x * 2 + half
    top, bottom = z == 7, z == 0
    first, second = half == 0, half == 1
    lead = (top & second) | (bottom & first)
    trail = (top & first) | (bottom & second)

    next_z, prev_z = (z + 1) % 8, (z + 7) % 8
    next_chip = choose(top, chip_of_row((row + 1) % 16), (x, y))
    prev_chip = choose(bottom, chip_of_row((row + 15) % 16), (x, y))
    has_next, has_prev = ~(top & (row == 15)), ~(bottom & (row == 0))
    partner = device_at(x, (y + 2) % 4, z, core)
    twin = device_at(x, y, z, 1 - core)
    following, following_cross = (device_at(*next_chip, next_z, c) for c in (core, 1 - core))
    preceding, preceding_cross = (device_at(*prev_chip, prev_z, c) for c in (core, 1 - core))

    end = top | bottom
    end_z = jnp.where(top, 0, 7)
    end_chip = choose(top, next_chip, prev_chip)
    has_end = jnp.where(top, has_next, has_prev) & end
    partner_row = row + 1 - 2 * half
    step = jnp.where(top, 1, 15)
    partner_end = chip_of_row((partner_row + step) % 16)
    partner_has_end = end & ~(top & (partner_row == 15)) & ~(bottom & (partner_row == 0))
    goal, goal_cross = (device_at(*partner_end, end_z, c) for c in (core, 1 - core))
    origin, origin_cross = (device_at(*flip(end_chip), end_z, c) for c in (core, 1 - core))
    chain_end, chain_end_cross = (device_at(*end_chip, end_z, c) for c in (core, 1 - core))

    bend = (top & (row == 7)) | (bottom & (row == 8))
    partner_bend = (top & (partner_row == 7)) | (bottom & (partner_row == 8))
    bend_relay = (top & (row == 14)) | (bottom & (row == 1))
    relay_to = device_at(x, (y + jnp.where(bend, jnp.where(top, 3, 1), 2)) % 4, z, core)
    relay_goal = choose(bend_relay, chip_of_row(jnp.where(top, 8, 7)), partner_end)
    relay_goal = device_at(*relay_goal, end_z, core)
    bend_sender = device_at(*chip_of_row(jnp.where(top, 7, 8)), z, core)
    bend_source = device_at(*chip_of_row(jnp.where(top, 1, 14)), end_z, core)
    crosses = (top & (core == 1)) | (bottom & (core == 0))

    def copy_in(kind, source):
        return pltpu.make_async_copy(source.at[half], mine.at[1 + half, kind], keep_sem.at[kind])

    kinds = ((L, lower), (U, upper), (F, rhs))
    for kind, source in kinds:
        copy_in(kind, source).start()

    barrier = pltpu.get_barrier_semaphore()

    def greet(device, condition):
        @pl.when(condition)
        def _():
            pl.semaphore_signal(barrier, inc=1, device_id=device, device_id_type=MESH)

    greet(partner, core < 2)
    greet(twin, core < 2)
    greet(following, ~top)
    greet(preceding, ~bottom)
    greet(following_cross, ~top & (core == 1))
    greet(preceding_cross, ~bottom & (core == 0))
    greet(chain_end, has_end & lead)
    greet(origin, has_end)
    greet(bend_sender, bend_relay)
    greet(bend_source, bend)
    greet(origin_cross, has_end & lead & crosses)
    greet(chain_end_cross, has_end & trail & crosses)
    expected = (
        ~top,
        ~bottom,
        ~top & (core == 1),
        ~bottom & (core == 0),
        has_end & lead,
        bend,
        bend_relay,
        partner_has_end,
        partner_has_end & trail & crosses,
        has_end & trail & crosses,
    )
    pl.semaphore_wait(barrier, 2 + sum(flag.astype(jnp.int32) for flag in expected))

    sent = []

    def only(condition, action):
        if condition is None:
            action()
        else:
            pl.when(condition)(action)

    gate = [None]

    def gated(condition):
        if gate[0] is None:
            return condition
        return gate[0] if condition is None else gate[0] & condition

    def send(source, target, send_sem, recv_sem, device, condition=None):
        condition = gated(condition)
        copy = pltpu.make_async_remote_copy(
            src_ref=source,
            dst_ref=target,
            send_sem=send_sem,
            recv_sem=recv_sem,
            device_id=device,
            device_id_type=MESH,
        )
        only(condition, copy.start)
        sent.append((condition, copy))

    def arrive(target, recv_sem, condition=None):
        condition = gated(condition)
        copy = pltpu.make_async_remote_copy(
            src_ref=target,
            dst_ref=target,
            send_sem=recv_sem,
            recv_sem=recv_sem,
            device_id=twin,
            device_id_type=MESH,
        )
        only(condition, copy.wait_recv)

    def to_mine(source, slot, kind, index, send_sem, device, condition):
        send(
            source,
            piece(mine.at[slot, kind], kind, index),
            send_sem,
            mine_recv.at[slot, kind, index],
            device,
            condition,
        )

    def to_near(source, slot, kind, index, send_sem, device, condition=None):
        send(
            source,
            piece(near.at[slot, kind], kind, index),
            send_sem,
            near_recv.at[slot, kind, index],
            device,
            condition,
        )

    mine_end = jnp.where(top, 0, 3)
    near_end = jnp.where(top, 0, 4)

    def reaches(kind, upward):
        return kind == F or (kind == U) == upward

    def start(kind):
        source = kinds[kind][1]
        for index in range(PIECES):
            other = piece(source.at[1 - half], kind, index)
            to_mine(other, 1 + half, kind, index, in_send.at[kind, index], partner, None)
            to_mine(other, mine_end, kind, index, extra_send.at[0, kind, index], goal, lead)
            if (kind, index) in BENT:
                send(
                    piece(source.at[half], kind, index),
                    piece(relay.at[kind], kind, index),
                    relay_send.at[0, kind, index],
                    relay_recv.at[kind, index],
                    relay_to,
                    lead & has_end if (kind, index) in RELAYED else bend,
                )
            for upward, side in ((True, top), (False, bottom)):
                if reaches(kind, upward):
                    to_near(
                        other,
                        0 if upward else 4,
                        kind,
                        index,
                        extra_send.at[1 if upward else 2, kind, index],
                        goal_cross,
                        trail & partner_has_end & crosses & side,
                    )

    first_slice = (row == 0) & bottom & (core == 0)
    last_slice = (row == 15) & top & (core == 1)

    def blank(ref, condition):
        condition = gated(condition)

        @pl.when(condition)
        def _():
            ref[...] = jnp.zeros(ref.shape, ref.dtype)

    blank(mine.at[0], ~has_prev)
    blank(mine.at[3], ~has_next)
    blank(near.at[0], ~has_prev & (core == 0))
    blank(near.at[4], ~has_next & (core == 1))

    def cut(slot, kind, part):
        if kind != F:
            blank(part, (first_slice & (slot == 1)) if kind == L else (last_slice & (slot == 2)))

    def pass_on(slot, kind, index, local):
        part = piece(mine.at[slot, kind], kind, index)
        number = 0 if local else 1
        to_near(part, slot + core, kind, index, twin_send.at[number, kind, index], twin)
        upward = second if local else first
        if local:
            bent = ~bend if (kind, index) in BENT else None
            chain = ~lead if (kind, index) in RELAYED else bent
        else:
            chain = ~trail
        for way, device, there, target in (
            (upward, following, has_next, 0),
            (~upward, preceding, has_prev, 3),
        ):
            condition = way & there if chain is None else way & there & chain
            to_mine(part, target, kind, index, chain_send.at[number, target // 3, kind, index], device, condition)
        cross = (core != half) if local else (core == half) & ~lead
        for way, device, there, target in (
            (core == 1, following_cross, has_next, 0),
            (core == 0, preceding_cross, has_prev, 4),
        ):
            if reaches(kind, target == 0):
                to_near(
                    part,
                    target,
                    kind,
                    index,
                    cross_send.at[number, target // 4, kind, index],
                    device,
                    way & there & cross,
                )

    def local(kind):
        copy_in(kind, kinds[kind][1]).wait()
        cut(1 + half, kind, mine.at[1 + half, kind])
        for index in range(PIECES):
            pass_on(1 + half, kind, index, True)

    def forward(kind, index):
        part = piece(mine.at[2 - half, kind], kind, index)
        arrive(part, mine_recv.at[2 - half, kind, index])
        cut(2 - half, kind, part)
        pass_on(2 - half, kind, index, False)
        if (kind, index) in BENT:
            part = piece(relay.at[kind], kind, index)
            waiting = bend_relay
            if (kind, index) in RELAYED:
                waiting |= trail & partner_has_end & ~partner_bend
            arrive(part, relay_recv.at[kind, index], waiting)
            to_mine(part, mine_end, kind, index, relay_send.at[1, kind, index], relay_goal, waiting)

    def halo(kind, index):
        for slot, there in ((0, has_prev), (3, has_next)):
            part = piece(mine.at[slot, kind], kind, index)
            arrive(part, mine_recv.at[slot, kind, index], there)
            upward = slot == 0
            condition = None if reaches(kind, upward) else (core == 1) if upward else (core == 0)
            to_near(
                part, slot + core, kind, index, halo_send.at[slot // 3, kind, index], twin, condition
            )

    def settle(slot, kind, index):
        if slot in (0, 4) and not reaches(kind, slot == 0):
            return
        condition = {0: (core == 1) | has_prev, 4: (core == 0) | has_next}.get(slot)
        arrive(piece(near.at[slot, kind], kind, index), near_recv.at[slot, kind, index], condition)

    def settle_blocks(*slots):
        for slot in slots:
            for kind in (L, U):
                for index in range(PIECES):
                    settle(slot, kind, index)

    def horner(jobs):
        for step in range(3):
            for number, (matrix, values, store) in enumerate(jobs):
                width = values.shape[1]
                last = values if step == 0 else inner.at[number, step - 1, :, pl.ds(0, width)]
                target = store if step == 2 else inner.at[number, step, :, pl.ds(0, width)]
                target[...] = (values[...].astype(jnp.float32) + dot(matrix[...], last[...])).astype(
                    jnp.bfloat16
                )

    def correct(k):
        corr[k] = (dot(mine[k, L], near[k, U]) + dot(mine[k, U], near[k + 1, L])).astype(jnp.bfloat16)

    def couple_left(k):
        left_terms[k] = (-dot(mine[k, L], near[k, L])).astype(jnp.bfloat16)
        return corr.at[k], left_terms.at[k], left_one.at[k]

    def couple_right(k):
        right_terms[k] = (-dot(mine[k, U], near[k + 1, U])).astype(jnp.bfloat16)
        return corr.at[k], right_terms.at[k], right_one.at[k]

    def source(values, left, right, before, after, span):
        return (
            values[:, span].astype(jnp.float32)
            - dot(left[...], before[:, span])
            - dot(right[...], after[:, span])
        ).astype(jnp.bfloat16)

    def forward_if(condition, index):
        gate[0] = condition
        forward(F, index)
        gate[0] = None

    def settle_if(condition, *slots):
        gate[0] = condition
        settle_blocks(*slots)
        gate[0] = None

    every = range(PIECES)
    inside = ~end
    start(L)
    local(L)
    start(U)
    local(U)
    start(F)
    for kind in (L, U):
        for index in every:
            forward(kind, index)
    local(F)
    for index in every:
        halo(L, index)
    settle_blocks(2)
    settle_if(core == 0, 3)
    settle_if(core == 1, 1)
    k = 2 - core
    correct(k)
    horner([couple_left(k), couple_right(k)])
    forward_if(inside, 0)
    forward_if(inside, 1)
    for index in every:
        halo(U, index)
    forward_if(end, 0)
    settle_if(core == 0, 1)
    settle_if(core == 1, 3)
    k = 1 + core
    correct(k)
    horner([couple_left(k), couple_right(k)])
    forward_if(inside, 2)
    forward_if(end, 1)
    settle_blocks(0, 4)
    correct(0)
    correct(3)
    horner([couple_right(0), couple_left(3)])
    forward_if(inside, 3)
    forward_if(end, 2)

    for k in (1, 2):
        corr[3 + k] = (
            dot(left_one[k], right_one[k - 1]) + dot(right_one[k], left_one[k + 1])
        ).astype(jnp.bfloat16)

    def home_copy(slot, index):
        return pltpu.make_async_copy(
            piece(result.at[slot], F, index), piece(out.at[half], F, index), keep_sem.at[3 + index]
        )

    def send_out(slot, index):
        pl.when(half == slot)(home_copy(slot, index).start)
        send(
            piece(result.at[slot], F, index),
            piece(out.at[half], F, index),
            out_send.at[index],
            out_recv.at[index],
            partner,
            half != slot,
        )

    for columns in COLUMNS:
        span = pl.ds(*columns)
        indices = range(columns[0] // PIECE, (columns[0] + columns[1]) // PIECE)
        for index in indices:
            halo(F, index)
        if columns[0] == 0:
            forward_if(end, 3)
        for index in indices:
            for slot in range(5):
                settle(slot, F, index)
        jobs = []
        for k in range(4):
            sources[k, :, span] = source(
                mine.at[k, F], mine.at[k, L], mine.at[k, U], near.at[k, F], near.at[k + 1, F], span
            )
            jobs.append((corr.at[k], sources.at[k, :, span], fields.at[k, :, span]))
        horner(jobs)
        jobs = []
        for slot in (0, 1):
            k = slot + 1
            sources[k, :, span] = source(
                fields.at[k], left_one.at[k], right_one.at[k], fields.at[k - 1], fields.at[k + 1], span
            )
            jobs.append((corr.at[3 + k], sources.at[k, :, span], result.at[slot, :, span]))
        horner(jobs)
        for slot in (0, 1):
            for index in indices:
                send_out(slot, index)
    for condition, copy in sent:
        only(condition, copy.wait_send)
    for index in range(PIECES):
        for slot in (0, 1):
            pl.when(half == slot)(home_copy(slot, index).wait)
        arrive(piece(out.at[1 - half], F, index), out_recv.at[index])


def on_device(lower, upper, rhs):
    blocks = lambda *lead: pltpu.VMEM((*lead, W, W), jnp.bfloat16)
    copies = lambda *lead: pltpu.SemaphoreType.DMA(lead)
    hbm = pl.BlockSpec(memory_space=pltpu.HBM)
    reduced = pl.pallas_call(
        kernel,
        out_shape=jax.ShapeDtypeStruct((2, W, W), jnp.bfloat16),
        in_specs=[hbm] * 3,
        out_specs=pl.BlockSpec(memory_space=pl.ANY),
        scratch_shapes=[
            blocks(4, 3),
            blocks(5, 3),
            blocks(3),
            blocks(6),
            blocks(4),
            blocks(4),
            blocks(4),
            blocks(4),
            blocks(4),
            blocks(4),
            blocks(4, 2),
            blocks(2),
            copies(3 + PIECES),
            copies(3, PIECES),
            copies(2, 3, PIECES),
            copies(3, PIECES),
            copies(3, 3, PIECES),
            copies(4, 3, PIECES),
            copies(5, 3, PIECES),
            copies(2, 3, PIECES),
            copies(2, 2, 3, PIECES),
            copies(2, 2, 3, PIECES),
            copies(2, 3, PIECES),
            copies(PIECES),
            copies(PIECES),
        ],
        compiler_params=pltpu.CompilerParams(
            collective_id=0, has_side_effects=True, vmem_limit_bytes=60 * 2**20
        ),
    )(lower[:, 0], upper[:, 0], rhs[:, 0])
    return reduced.astype(jnp.float32)[:, None]


def solution(mesh):
    return jax.shard_map(
        on_device,
        mesh=mesh,
        in_specs=(P("col", "cuts", None, None),) * 3,
        out_specs=P("col", "cuts", None, None),
        check_vma=False,
    )
```
